32 devices in a mesh: fsdp: 4 (over y, x), tensor: 8 (over z, core).
Axes of the slice: x: 2, y: 2, z: 4, core: 2. Of those that a mesh axis runs over, the one named last changes fastest.
Arguments:
- inputs: bfloat16 [768, 8192], P('fsdp'), may hold values from -6 to 6
- cotangent: bfloat16 [768, 8192], P('fsdp'), may hold values from -1.1953125 to 1.1953125
- up_tiles: bfloat16 [8, 16, 128, 128], P('tensor', 'fsdp'), may hold values from -0.75 to 0.75
- up_rows: int32 [8, 16], P('tensor', 'fsdp'), may hold values from 0 to 63, as said below
- up_cols: int32 [8, 16], P('tensor', 'fsdp'), may hold values from 0 to 31, as said below
- down_tiles: bfloat16 [8, 16, 128, 128], P('tensor', 'fsdp'), may hold values from -0.75 to 0.75
- down_rows: int32 [8, 16], P('tensor', 'fsdp'), may hold values from 0 to 31, as said below
- down_cols: int32 [8, 16], P('tensor', 'fsdp'), may hold values from 0 to 63, as said below
Outputs:
- input_grad: bfloat16 [768, 8192], P('fsdp', 'tensor')
- up_grad: bfloat16 [8, 16, 128, 128], P('tensor', 'fsdp')
- down_grad: bfloat16 [8, 16, 128, 128], P('tensor', 'fsdp')
The draws below stay inside these ranges and needn't reach their ends.
Inputs may be any that keep to these rules, and one draw needn't show every extreme that they name: `up_rows`: together with up_cols, the positions of a group's 16 tiles are distinct; slot s is held by fsdp index s // 4. `up_cols`: see up_rows. `down_rows`: together with down_cols, the positions of a group's 16 tiles are distinct; slot s is held by fsdp index s // 4. `down_cols`: see down_rows.
All inputs are finite; a program needn't handle non-finite values.
Results may differ from the reference program's by a relative error of at most 0.015.
Values may be sent and summed in bfloat16 or wider, within the bound.
No kernel may reach another device: no remote copies, remote signals or barrier semaphores. Data moves between devices by JAX's collectives and lax.ppermute only.
A program may use at most 128 MiB of HBM per device.

```python
import jax
import jax.numpy as jnp
from jax import lax

D = 8192
TILE = 128
TOK_DEV = 192
TOKENS = 768
GROUPS = 8
SLOTS = 16
ROW_BLOCKS = 64
GROUP_COLS = 32
N_FSDP = 4


def tile_positions(key, row_count, col_count):
    total = row_count * col_count

    def one_group(group_key):
        first_key, second_key = jax.random.split(group_key)
        middle = (jax.random.permutation(first_key, total - 2) + 1).astype(jnp.int32)
        ends = jnp.array([0, total - 1], jnp.int32)
        picked = jnp.concatenate([ends, middle[:SLOTS - 2]])
        order = jax.random.permutation(second_key, SLOTS)
        return picked[order]
    keys = jax.random.split(key, GROUPS)
    return jax.vmap(one_group)(keys)


def draw_up_rows(key, part):
    places = tile_positions(jax.random.fold_in(key, 11), ROW_BLOCKS, GROUP_COLS)
    return (places // GROUP_COLS).astype(jnp.int32)


def draw_up_cols(key, part):
    places = tile_positions(jax.random.fold_in(key, 11), ROW_BLOCKS, GROUP_COLS)
    return (places % GROUP_COLS).astype(jnp.int32)


def draw_down_rows(key, part):
    places = tile_positions(jax.random.fold_in(key, 23), GROUP_COLS, ROW_BLOCKS)
    return (places // ROW_BLOCKS).astype(jnp.int32)


def draw_down_cols(key, part):
    places = tile_positions(jax.random.fold_in(key, 23), GROUP_COLS, ROW_BLOCKS)
    return (places % ROW_BLOCKS).astype(jnp.int32)


def block_levels(rng, extent, cuts, low, high):
    loudness, own = 1.0, jax.random.fold_in(rng, 6)
    for axis_at, shards_of in cuts:
        draws = jnp.exp(jax.random.uniform(jax.random.fold_in(own, axis_at), (shards_of,), jnp.float32, low / len(cuts), high / len(cuts)))
        loudness = loudness * jnp.repeat(draws, extent[axis_at] // shards_of).reshape([-1 if axis == axis_at else 1 for axis in range(len(extent))])
    return loudness


def scatter_about(own_key, extent, scale, reach, shards=(), kind=jnp.bfloat16):
    factor_of = block_levels(own_key, extent, shards, -0.22, 0.18) if shards else 1.0
    entries = jax.random.normal(own_key, extent, jnp.float32) * scale * factor_of
    return jnp.minimum(jnp.maximum(entries, -reach), reach).astype(kind)


def setup_inputs(seed: int = 0) -> dict:
    arg_keys = jax.random.split(jax.random.key(seed), 9)
    inputs = scatter_about(arg_keys[0], (TOKENS, D), 1.0, 6.0, ((0, 4),))
    cotangent = scatter_about(arg_keys[1], (TOKENS, D), 0.2, 1.1953125, ((0, 4),))
    up_tiles = scatter_about(arg_keys[2], (GROUPS, SLOTS, TILE, TILE), (TILE * SLOTS // GROUP_COLS) ** -0.5, 0.75, ((0, 8), (1, 4)))
    up_rows = draw_up_rows(jax.random.fold_in(arg_keys[8], 71), 0)
    up_cols = draw_up_cols(jax.random.fold_in(arg_keys[8], 71), 0)
    down_tiles = scatter_about(arg_keys[5], (GROUPS, SLOTS, TILE, TILE), (TILE * SLOTS // GROUP_COLS) ** -0.5, 0.75, ((0, 8), (1, 4)))
    down_rows = draw_down_rows(jax.random.fold_in(arg_keys[8], 71), 0)
    down_cols = draw_down_cols(jax.random.fold_in(arg_keys[8], 71), 0)
    return dict(inputs=inputs, cotangent=cotangent, up_tiles=up_tiles, up_rows=up_rows, up_cols=up_cols, down_tiles=down_tiles, down_rows=down_rows, down_cols=down_cols)


def gelu_parts(pre):
    coef = 0.7978845608028654
    inner = coef * (pre + 0.044715 * pre * pre * pre)
    tanh_val = jnp.tanh(inner)
    act = 0.5 * pre * (1.0 + tanh_val)
    slope = 0.5 * (1.0 + tanh_val) + 0.5 * pre * (1.0 - tanh_val * tanh_val) * coef * (1.0 + 3.0 * 0.044715 * pre * pre)
    return act, slope


def reference(inputs, cotangent, up_tiles, up_rows, up_cols, down_tiles, down_rows, down_cols):
    tok_count = inputs.shape[0]
    input_blocks = inputs.reshape(tok_count, ROW_BLOCKS, TILE)
    cotan_blocks = cotangent.reshape(tok_count, ROW_BLOCKS, TILE)

    def group_step(carry, group):
        w_up, r_up, c_up, w_down, r_down, c_down = group
        x_sel = jnp.take(input_blocks, r_up, axis=1).astype(jnp.float32)
        prod = jnp.einsum("tsk,skf->stf", x_sel, w_up.astype(jnp.float32))
        pre = jax.ops.segment_sum(prod, c_up, num_segments=GROUP_COLS)
        act, slope = gelu_parts(pre)
        hidden = act.astype(jnp.bfloat16)
        dy_sel = jnp.take(cotan_blocks, c_down, axis=1).astype(jnp.float32)
        back = jnp.einsum("tsk,sfk->stf", dy_sel, w_down.astype(jnp.float32))
        dhid = jax.ops.segment_sum(back, r_down, num_segments=GROUP_COLS)
        dpre = (dhid * slope).astype(jnp.bfloat16)
        h_sel = jnp.take(hidden, r_down, axis=0).astype(jnp.float32)
        h_split = h_sel.reshape(SLOTS, N_FSDP, TOK_DEV, TILE)
        dy_split = dy_sel.reshape(N_FSDP, TOK_DEV, SLOTS, TILE)
        down_part = jnp.einsum("sbtf,btsk->bsfk", h_split, dy_split).astype(jnp.bfloat16)
        down_grad = jnp.sum(down_part.astype(jnp.float32), axis=0).astype(jnp.bfloat16)
        dp_sel = jnp.take(dpre, c_up, axis=0).astype(jnp.float32)
        dp_split = dp_sel.reshape(SLOTS, N_FSDP, TOK_DEV, TILE)
        x_split = x_sel.reshape(N_FSDP, TOK_DEV, SLOTS, TILE)
        up_part = jnp.einsum("btsk,sbtf->bskf", x_split, dp_split).astype(jnp.bfloat16)
        up_grad = jnp.sum(up_part.astype(jnp.float32), axis=0).astype(jnp.bfloat16)
        back_in = jnp.einsum("stf,skf->stk", dp_sel, w_up.astype(jnp.float32))
        in_part = jax.ops.segment_sum(back_in, r_up, num_segments=ROW_BLOCKS).astype(jnp.bfloat16)
        return carry + in_part.astype(jnp.float32), (up_grad, down_grad)

    start = jnp.zeros((ROW_BLOCKS, tok_count, TILE), jnp.float32)
    total, grads = lax.scan(group_step, start, (up_tiles, up_rows, up_cols, down_tiles, down_rows, down_cols))
    input_grad = jnp.transpose(total, (1, 0, 2)).reshape(tok_count, D).astype(jnp.bfloat16)
    return input_grad, grads[0], grads[1]
```

```python
import functools

import jax
import jax.numpy as jnp
from jax import lax
from jax.experimental import pallas as pl
from jax.experimental.pallas import tpu as pltpu
from jax.sharding import PartitionSpec as P

FF = 32768
TILE = 128
IDX_ROWS = 16
BF16 = jnp.bfloat16
F32 = jnp.float32

VMEM = pl.BlockSpec(memory_space=pltpu.VMEM)
SMEM = pl.BlockSpec(memory_space=pltpu.SMEM)
ANY = pl.BlockSpec(memory_space=pl.ANY)


def gelu_parts(pre):
    coef = 0.7978845608028654
    sq = pre * pre
    tanh_val = jnp.tanh(coef * (pre + 0.044715 * pre * sq))
    half = 0.5 * (1.0 + tanh_val)
    act = pre * half
    slope = half + 0.5 * pre * (1.0 - tanh_val * tanh_val) * coef * (
        1.0 + 3.0 * 0.044715 * sq
    )
    return (act, slope)


def pack_kernel(up_ref, down_ref, ur_ref, uc_ref, dr_ref, dc_ref, out_ref):
    held = up_ref.shape[0] // TILE
    rows = up_ref.shape[0]
    out_ref[:rows] = up_ref[...]
    out_ref[rows : 2 * rows] = down_ref[...]
    lane = lax.broadcasted_iota(jnp.int32, (IDX_ROWS, TILE), 1)
    val = jnp.zeros((IDX_ROWS, TILE), jnp.int32)
    for kind, ref in enumerate((ur_ref, uc_ref, dr_ref, dc_ref)):
        for i in range(held):
            val = jnp.where(lane == kind * held + i, ref[0, i], val)
    out_ref[2 * rows :] = val.astype(F32).astype(BF16)


def dot(a, b, dims):
    return lax.dot_general(a, b, (dims, ((), ())), preferred_element_type=F32)


def main_kernel(n_f, held, n_z, per_dev, z_ref, x_ref, dy_ref, *refs):
    packs = refs[:n_f]
    mine = refs[n_f : n_f + n_z]
    other = refs[n_f + n_z : n_f + 2 * n_z]
    xs, dys, dps, hs = refs[n_f + 2 * n_z : n_f + 2 * n_z + 4]
    pre, dhid, hid, dpre, acc, idx_v, idx, flag, sem_i, sem_x, sem_y = refs[
        n_f + 2 * n_z + 4 :
    ]
    slots = n_f * held
    rows = held * TILE
    z, core = z_ref[0], z_ref[1]
    for f in range(n_f):
        idx_v[f : f + 1] = packs[f][2 * rows :][:1].astype(F32).astype(jnp.int32)
    copy = pltpu.make_async_copy(idx_v, idx, sem_i)
    copy.start()
    copy.wait()

    def at(kind, s):
        return idx[s // held, kind * held + s % held]

    def block(ref, which, out, sem, s):
        col = pl.ds(pl.multiple_of(which * TILE, TILE), TILE)
        return pltpu.make_async_copy(ref.at[:, col], out.at[s], sem.at[s])

    for s in range(slots):
        block(x_ref, at(0, s), xs, sem_x, s).start()
        block(dy_ref, at(3, s), dys, sem_y, s).start()
    pre[...] = jnp.zeros_like(pre)
    dhid[...] = jnp.zeros_like(dhid)
    hid[...] = jnp.zeros_like(hid)
    acc[...] = jnp.zeros_like(acc)
    for c in range(pre.shape[0]):
        flag[c] = 0

    def up_tile(s):
        return packs[s // held][pl.ds((s % held) * TILE, TILE)]

    def down_tile(s):
        return packs[s // held][pl.ds(rows + (s % held) * TILE, TILE)]

    for s in range(slots):
        block(x_ref, at(0, s), xs, sem_x, s).wait()
        pre[at(1, s)] += dot(xs[s], up_tile(s), ((1,), (0,)))
    for s in range(slots):
        block(dy_ref, at(3, s), dys, sem_y, s).wait()
        dhid[at(2, s)] += dot(dys[s], down_tile(s), ((1,), (1,)))
    for s in range(slots):
        c = at(1, s)

        @pl.when(flag[c] == 0)
        def _():
            act, slope = gelu_parts(pre[c])
            hid[c] = act.astype(BF16)
            dpre[c] = (dhid[c] * slope).astype(BF16)
            flag[c] = 1

    for s in range(slots):
        dp = dpre[at(1, s)]
        dps[s] = dp
        hs[s] = hid[at(2, s)]
        r = at(0, s)
        dev, j = r // per_dev, r % per_dev
        to_z, to_core = dev // 2, dev % 2
        k = jnp.bitwise_xor(to_z, z) if n_z == 4 else to_z
        whose = jnp.bitwise_xor(to_core, core)
        col = pl.ds(pl.multiple_of(j * TILE, TILE), TILE)
        acc[whose * n_z + k, :, col] += dot(dp, up_tile(s), ((1,), (1,)))
    for k in range(n_z):
        mine[k][...] = acc[k].astype(BF16)
        other[k][...] = acc[n_z + k].astype(BF16)


def grad_kernel(n_f, held, xs, dys, dps, hs, *outs):
    for s in range(n_f * held):
        f, i = s // held, s % held
        outs[f][i] = dot(xs[s], dps[s], ((0,), (0,))).astype(BF16)
        outs[f][held + i] = dot(hs[s], dys[s], ((0,), (0,))).astype(BF16)


def vmem_limit(mb):
    return pltpu.CompilerParams(vmem_limit_bytes=mb * 1024 * 1024)


def on_device(inputs, cotangent, up_tiles, up_rows, up_cols, down_tiles, down_rows, down_cols):
    n_f, n_t = lax.axis_size("fsdp"), lax.axis_size("tensor")
    n_z = n_t // 2
    tok, width = inputs.shape
    per_dev = width // (n_t * TILE)
    group_cols = FF // (n_t * TILE)
    held = up_tiles.shape[1]
    rows = held * TILE
    slots = held * n_f
    t = lax.axis_index("tensor")
    z, core = t // 2, t % 2

    def over_f(a, k):
        return lax.ppermute(a, "fsdp", [(f, f ^ k) for f in range(n_f)])

    def over_t(a, k):
        return lax.ppermute(a, "tensor", [(i, i ^ k) for i in range(n_t)])

    pack = pl.pallas_call(
        pack_kernel,
        out_shape=jax.ShapeDtypeStruct((2 * rows + IDX_ROWS, TILE), BF16),
        in_specs=[VMEM, VMEM, SMEM, SMEM, SMEM, SMEM],
        out_specs=VMEM,
    )(
        up_tiles.reshape(rows, TILE),
        down_tiles.reshape(rows, TILE),
        up_rows,
        up_cols,
        down_rows,
        down_cols,
    )
    packs = [pack] + [over_f(pack, k) for k in range(1, n_f)]
    shard = jax.ShapeDtypeStruct((tok, per_dev * TILE), BF16)
    sel = jax.ShapeDtypeStruct((slots, tok, TILE), BF16)
    outs = pl.pallas_call(
        functools.partial(main_kernel, n_f, held, n_z, per_dev),
        out_shape=[shard] * (2 * n_z) + [sel] * 4,
        in_specs=[SMEM, ANY, ANY] + [VMEM] * n_f,
        out_specs=[VMEM] * (2 * n_z + 4),
        scratch_shapes=[
            pltpu.VMEM((group_cols, tok, TILE), F32),
            pltpu.VMEM((group_cols, tok, TILE), F32),
            pltpu.VMEM((group_cols, tok, TILE), BF16),
            pltpu.VMEM((group_cols, tok, TILE), BF16),
            pltpu.VMEM((2 * n_z, tok, per_dev * TILE), F32),
            pltpu.VMEM((n_f, TILE), jnp.int32),
            pltpu.SMEM((n_f, TILE), jnp.int32),
            pltpu.SMEM((group_cols,), jnp.int32),
            pltpu.SemaphoreType.DMA,
            pltpu.SemaphoreType.DMA((slots,)),
            pltpu.SemaphoreType.DMA((slots,)),
        ],
        compiler_params=vmem_limit(48),
    )(jnp.stack([z, core]).astype(jnp.int32), inputs, cotangent, *packs)
    mine, other = outs[:n_z], outs[n_z : 2 * n_z]
    chosen = outs[2 * n_z :]
    parts = [
        (m.astype(F32) + over_t(o, 1).astype(F32)).astype(BF16) for m, o in zip(mine, other)
    ]
    terms = pl.pallas_call(
        functools.partial(grad_kernel, n_f, held),
        out_shape=[jax.ShapeDtypeStruct((2 * held, TILE, TILE), BF16)] * n_f,
        in_specs=[VMEM] * 4,
        out_specs=[VMEM] * n_f,
        compiler_params=vmem_limit(48),
    )(*chosen)
    total = terms[0].astype(F32)
    for k in range(1, n_f):
        total = total + over_f(terms[k], k).astype(F32)
    total = total.astype(BF16)
    if n_z == 4:
        got = [parts[0]] + [over_t(parts[k], 2 * k) for k in range(n_z - 1, 0, -1)]
        input_grad = sum(g.astype(F32) for g in got).astype(BF16)
    else:
        input_grad = lax.psum_scatter(
            jnp.stack(parts),
            "tensor",
            scatter_dimension=0,
            tiled=False,
            axis_index_groups=[list(range(c, n_t, 2)) for c in range(2)],
        )
    return (input_grad, total[:held][None], total[held:][None])


def solution(mesh):
    placed = (
        P("fsdp", None),
        P("fsdp", None),
        P("tensor", "fsdp", None, None),
        P("tensor", "fsdp"),
        P("tensor", "fsdp"),
        P("tensor", "fsdp", None, None),
        P("tensor", "fsdp"),
        P("tensor", "fsdp"),
    )
    return jax.shard_map(
        on_device,
        mesh=mesh,
        in_specs=placed,
        out_specs=(
            P("fsdp", "tensor"),
            P("tensor", "fsdp", None, None),
            P("tensor", "fsdp", None, None),
        ),
        check_vma=False,
    )
```

```python
import functools

import jax
import jax.numpy as jnp
from jax import lax
from jax.experimental import pallas as pl
from jax.experimental.pallas import tpu as pltpu
from jax.sharding import PartitionSpec as P

FF = 32768
TILE = 128
IDX_ROWS = 16
BF16 = jnp.bfloat16
F32 = jnp.float32

VMEM = pl.BlockSpec(memory_space=pltpu.VMEM)
SMEM = pl.BlockSpec(memory_space=pltpu.SMEM)
ANY = pl.BlockSpec(memory_space=pl.ANY)
HBM = pl.BlockSpec(memory_space=pltpu.HBM)


def gelu_parts(pre):
    coef = 0.7978845608028654
    sq = pre * pre
    tanh_val = jnp.tanh(coef * (pre + 0.044715 * pre * sq))
    half = 0.5 * (1.0 + tanh_val)
    act = pre * half
    slope = half + 0.5 * pre * (1.0 - tanh_val * tanh_val) * coef * (
        1.0 + 3.0 * 0.044715 * sq
    )
    return (act, slope)


def pack(up_ref, places, out_ref):
    held = up_ref.shape[0]
    out_ref[: held * TILE] = up_ref[...].reshape(held * TILE, TILE)
    lane = lax.broadcasted_iota(jnp.int32, (IDX_ROWS, TILE), 1)
    val = jnp.zeros((IDX_ROWS, TILE), jnp.int32)
    for kind, ref in enumerate(places):
        for i in range(held):
            val = jnp.where(lane == kind * held + i, ref[0, i], val)
    out_ref[held * TILE :] = val.astype(F32).astype(BF16)


def pack_kernel(ur, uc, dr, dc, up, out):
    pack(up, (ur, uc, dr, dc), out)


def fetch_kernel(x, dy, x_out, dy_out, sem):
    copies = [
        pltpu.make_async_copy(x, x_out, sem.at[0]),
        pltpu.make_async_copy(dy, dy_out, sem.at[1]),
    ]
    for copy in copies:
        copy.start()
    for copy in copies:
        copy.wait()


def vmem_limit(mb):
    return pltpu.CompilerParams(vmem_limit_bytes=mb * 1024 * 1024)


def dot(a, b, dims):
    return lax.dot_general(a, b, (dims, ((), ())), preferred_element_type=F32)


def main_kernel(n_f, held, n_z, per_dev, z_ref, x_ref, dy_ref, *refs):
    ups, downs = refs[:n_f], refs[n_f : 2 * n_f]
    refs = refs[2 * n_f :]
    mine, other = refs[:n_z], refs[n_z : 2 * n_z]
    xs, dys, dps, hs = refs[2 * n_z : 2 * n_z + 4]
    (prod, back, rprod, hid, dpre, out, idx_v, idx, first, d_first, r_first, lead, sem_i) = refs[
        2 * n_z + 4 :
    ]
    slots = n_f * held
    z, core = z_ref[0], z_ref[1]
    for f in range(n_f):
        idx_v[f : f + 1] = ups[f][held * TILE :][:1].astype(F32).astype(jnp.int32)
    copy = pltpu.make_async_copy(idx_v, idx, sem_i)
    copy.start()
    copy.wait()

    def at(kind, s):
        return idx[s // held, kind * held + s % held]

    def block(ref, which):
        return ref[:, pl.ds(pl.multiple_of(which * TILE, TILE), TILE)]

    out[...] = jnp.zeros_like(out)
    back[slots] = jnp.zeros_like(back[slots])
    hid[slots] = jnp.zeros_like(hid[slots])
    for table, kind in ((first, 1), (d_first, 2), (r_first, 0)):
        for c in range(table.shape[0]):
            table[c] = -1
        for s in range(slots):
            c = at(kind, s)
            seen = table[c]
            leader = jnp.where(seen < 0, s, seen)
            table[c] = leader
            lead[kind, s] = leader

    def up_tile(s):
        return ups[s // held][pl.ds((s % held) * TILE, TILE)]

    def down_tile(s):
        return downs[s // held][s % held]

    def fold(buf, kind):
        for s in range(1, slots):
            leader = lead[kind, s]

            @pl.when(leader != s)
            def _():
                buf[leader] += buf[s]

    for s in range(slots):
        x = block(x_ref, at(0, s))
        xs[s] = x
        prod[s] = dot(x, up_tile(s), ((1,), (0,)))
    for s in range(slots):
        dy = block(dy_ref, at(3, s))
        dys[s] = dy
        back[s] = dot(dy, down_tile(s), ((1,), (1,)))
    fold(prod, 1)
    fold(back, 2)
    for s in range(slots):

        @pl.when(lead[1, s] == s)
        def _():
            act, slope = gelu_parts(prod[s])
            d = d_first[at(1, s)]
            hid[s] = act.astype(BF16)
            dpre[s] = (back[jnp.where(d < 0, slots, d)] * slope).astype(BF16)

    for s in range(slots):
        dp = dpre[lead[1, s]]
        dps[s] = dp
        rprod[s] = dot(dp, up_tile(s), ((1,), (1,)))
        h = first[at(2, s)]
        hs[s] = hid[jnp.where(h < 0, slots, h)]
    fold(rprod, 0)
    for s in range(slots):

        @pl.when(lead[0, s] == s)
        def _():
            r = at(0, s)
            dev, j = r // per_dev, r % per_dev
            to_z, to_core = dev // 2, dev % 2
            k = n_z - 1 - jnp.bitwise_xor(to_z, z) if n_z == 4 else to_z
            whose = jnp.bitwise_xor(to_core, core)
            col = pl.ds(pl.multiple_of(j * TILE, TILE), TILE)
            out[whose * n_z + k, :, col] = rprod[s].astype(BF16)

    for k in range(n_z):
        mine[k][...] = out[k]
        other[k][...] = out[n_z + k]


def add_kernel(a, b, out):
    out[...] = a[...].astype(F32) + b[...].astype(F32)


def main_call(n_f, held, n_z, per_dev, group_cols, place, inputs, cotangent, tiles):
    tok, width = inputs.shape
    slots = n_f * held
    shard = jax.ShapeDtypeStruct((tok, per_dev * TILE), BF16)
    sel = jax.ShapeDtypeStruct((slots, tok, TILE), BF16)
    return pl.pallas_call(
        functools.partial(main_kernel, n_f, held, n_z, per_dev),
        out_shape=[shard] * (2 * n_z) + [sel] * 4,
        in_specs=[SMEM] + [VMEM] * (2 + 2 * n_f),
        out_specs=[VMEM] * (2 * n_z + 4),
        scratch_shapes=[
            pltpu.VMEM((slots, tok, TILE), F32),
            pltpu.VMEM((slots + 1, tok, TILE), F32),
            pltpu.VMEM((slots, tok, TILE), F32),
            pltpu.VMEM((slots + 1, tok, TILE), BF16),
            pltpu.VMEM((slots, tok, TILE), BF16),
            pltpu.VMEM((2 * n_z, tok, per_dev * TILE), BF16),
            pltpu.VMEM((n_f, TILE), jnp.int32),
            pltpu.SMEM((n_f, TILE), jnp.int32),
            pltpu.SMEM((group_cols,), jnp.int32),
            pltpu.SMEM((group_cols,), jnp.int32),
            pltpu.SMEM((width // TILE,), jnp.int32),
            pltpu.SMEM((3, slots), jnp.int32),
            pltpu.SemaphoreType.DMA,
        ],
        compiler_params=vmem_limit(24 if slots <= 16 else 56),
    )(place, inputs, cotangent, *tiles)


def grad_kernel(n_f, held, after, xs, dys, dps, hs, *outs):
    for s in range(n_f * held):
        f, i = s // held, s % held
        outs[f][i] = dot(xs[s], dps[s], ((0,), (0,))).astype(BF16)
        outs[f][held + i] = dot(hs[s], dys[s], ((0,), (0,))).astype(BF16)


def on_device(inputs, cotangent, up_tiles, up_rows, up_cols, down_tiles, down_rows, down_cols):
    n_f, n_t = lax.axis_size("fsdp"), lax.axis_size("tensor")
    n_z = n_t // 2
    tok, width = inputs.shape
    per_dev = width // (n_t * TILE)
    group_cols = FF // (n_t * TILE)
    held = up_tiles.shape[1]
    rows = held * TILE
    slots = held * n_f
    t = lax.axis_index("tensor")
    z, core = t // 2, t % 2

    zc = jnp.stack([z, core]).astype(jnp.int32)

    def over_f(a, k):
        return lax.ppermute(a, "fsdp", [(f, f ^ k) for f in range(n_f)])

    def over_t(a, k):
        return lax.ppermute(a, "tensor", [(i, i ^ k) for i in range(n_t)])

    up, down = up_tiles[0], down_tiles[0]
    where = (up_rows, up_cols, down_rows, down_cols)
    packed = jax.ShapeDtypeStruct((held * TILE + IDX_ROWS, TILE), BF16)
    downs = [over_f(down, k) for k in range(1, n_f)]
    sent = pl.pallas_call(
        pack_kernel,
        out_shape=packed,
        in_specs=[SMEM] * 4 + [VMEM],
        out_specs=VMEM,
    )(*where, up)
    x_v, dy_v = pl.pallas_call(
        fetch_kernel,
        out_shape=[jax.ShapeDtypeStruct(inputs.shape, BF16)] * 2,
        in_specs=[HBM, HBM],
        out_specs=[VMEM, VMEM],
        scratch_shapes=[pltpu.SemaphoreType.DMA((2,))],
        compiler_params=vmem_limit(16),
    )(inputs, cotangent)
    ups = [over_f(sent, k) for k in range(1, n_f)]
    tiles = [sent] + ups + [down] + downs
    outs = main_call(
        n_f, held, n_z, per_dev, group_cols, zc, x_v, dy_v, tiles
    )
    mine, other = outs[:n_z], outs[n_z : 2 * n_z]
    chosen = outs[2 * n_z :]
    parts = [
        (m.astype(F32) + over_t(o, 1).astype(F32)).astype(BF16)
        for m, o in zip(mine, other)
    ]
    if n_z == 4:
        far, cross, near, own = parts
        passed = over_t(far, 2)
        came = over_t(near, 2)
        across = over_t((cross.astype(F32) + passed.astype(F32)).astype(BF16), 4)
        acc = pl.pallas_call(
            add_kernel,
            out_shape=jax.ShapeDtypeStruct(own.shape, F32),
            in_specs=[VMEM] * 2,
            out_specs=VMEM,
            compiler_params=vmem_limit(8),
        )(own, came)
        input_grad = (acc + across.astype(F32)).astype(BF16)
        gate = near
    else:
        input_grad = lax.psum_scatter(
            jnp.stack(parts),
            "tensor",
            scatter_dimension=0,
            tiled=False,
            axis_index_groups=[list(range(c, n_t, 2)) for c in range(2)],
        )
        gate = parts[0]
    terms = pl.pallas_call(
        functools.partial(grad_kernel, n_f, held),
        out_shape=[jax.ShapeDtypeStruct((2 * held, TILE, TILE), BF16)] * n_f,
        in_specs=[ANY] + [VMEM] * 4,
        out_specs=[VMEM] * n_f,
        compiler_params=vmem_limit(16),
    )(gate, *chosen)
    total = terms[0].astype(F32)
    for k in range(1, n_f):
        total = total + over_f(terms[k], k).astype(F32)
    total = total.astype(BF16)
    return (input_grad, total[:held][None], total[held:][None])


def solution(mesh):
    placed = (
        P("fsdp", None),
        P("fsdp", None),
        P("tensor", "fsdp", None, None),
        P("tensor", "fsdp"),
        P("tensor", "fsdp"),
        P("tensor", "fsdp", None, None),
        P("tensor", "fsdp"),
        P("tensor", "fsdp"),
    )
    return jax.shard_map(
        on_device,
        mesh=mesh,
        in_specs=placed,
        out_specs=(
            P("fsdp", "tensor"),
            P("tensor", "fsdp", None, None),
            P("tensor", "fsdp", None, None),
        ),
        check_vma=False,
    )
```

```python
import functools

import jax
import jax.numpy as jnp
from jax import lax
from jax.experimental import pallas as pl
from jax.experimental.pallas import tpu as pltpu
from jax.sharding import PartitionSpec as P

FF = 32768
TILE = 128
IDX_ROWS = 16
BF16 = jnp.bfloat16
F32 = jnp.float32

VMEM = pl.BlockSpec(memory_space=pltpu.VMEM)
SMEM = pl.BlockSpec(memory_space=pltpu.SMEM)
ANY = pl.BlockSpec(memory_space=pl.ANY)
HBM = pl.BlockSpec(memory_space=pltpu.HBM)


def gelu_parts(pre):
    coef = 0.7978845608028654
    sq = pre * pre
    tanh_val = jnp.tanh(coef * (pre + 0.044715 * pre * sq))
    half = 0.5 * (1.0 + tanh_val)
    act = pre * half
    slope = half + 0.5 * pre * (1.0 - tanh_val * tanh_val) * coef * (
        1.0 + 3.0 * 0.044715 * sq
    )
    return (act, slope)


def pack(up_ref, places, out_ref):
    held = up_ref.shape[0]
    out_ref[: held * TILE] = up_ref[...].reshape(held * TILE, TILE)
    lane = lax.broadcasted_iota(jnp.int32, (IDX_ROWS, TILE), 1)
    val = jnp.zeros((IDX_ROWS, TILE), jnp.int32)
    for kind, ref in enumerate(places):
        for i in range(held):
            val = jnp.where(lane == kind * held + i, ref[0, i], val)
    out_ref[held * TILE :] = val.astype(F32).astype(BF16)


def pack_kernel(ur, uc, dr, dc, up, out):
    pack(up, (ur, uc, dr, dc), out)


def fetch_kernel(x, dy, x_out, dy_out, sem):
    copies = [
        pltpu.make_async_copy(x, x_out, sem.at[0]),
        pltpu.make_async_copy(dy, dy_out, sem.at[1]),
    ]
    for copy in copies:
        copy.start()
    for copy in copies:
        copy.wait()


def vmem_limit(mb):
    return pltpu.CompilerParams(vmem_limit_bytes=mb * 1024 * 1024)


def dot(a, b, dims):
    return lax.dot_general(a, b, (dims, ((), ())), preferred_element_type=F32)


def main_kernel(n_f, held, n_z, per_dev, z_ref, x_ref, dy_ref, *refs):
    ups, downs = refs[:n_f], refs[n_f : 2 * n_f]
    refs = refs[2 * n_f :]
    mine, other = refs[:n_z], refs[n_z : 2 * n_z]
    xs, dys, dps, hs = refs[2 * n_z : 2 * n_z + 4]
    (prod, back, rprod, hid, dpre, out, idx_v, idx, first, d_first, r_first, lead, sem_i) = refs[
        2 * n_z + 4 :
    ]
    slots = n_f * held
    z, core = z_ref[0], z_ref[1]
    for f in range(n_f):
        idx_v[f : f + 1] = ups[f][held * TILE :][:1].astype(F32).astype(jnp.int32)
    copy = pltpu.make_async_copy(idx_v, idx, sem_i)
    copy.start()
    copy.wait()

    def at(kind, s):
        return idx[s // held, kind * held + s % held]

    def block(ref, which):
        return ref[:, pl.ds(pl.multiple_of(which * TILE, TILE), TILE)]

    out[...] = jnp.zeros_like(out)
    back[slots] = jnp.zeros_like(back[slots])
    hid[slots] = jnp.zeros_like(hid[slots])
    for table, kind in ((first, 1), (d_first, 2), (r_first, 0)):
        for c in range(table.shape[0]):
            table[c] = -1
        for s in range(slots):
            c = at(kind, s)
            seen = table[c]
            leader = jnp.where(seen < 0, s, seen)
            table[c] = leader
            lead[kind, s] = leader

    def up_tile(s):
        return ups[s // held][pl.ds((s % held) * TILE, TILE)]

    def down_tile(s):
        return downs[s // held][s % held]

    def fold(buf, kind):
        for s in range(1, slots):
            leader = lead[kind, s]

            @pl.when(leader != s)
            def _():
                buf[leader] += buf[s]

    for s in range(slots):
        x = block(x_ref, at(0, s))
        xs[s] = x
        prod[s] = dot(x, up_tile(s), ((1,), (0,)))
    for s in range(slots):
        dy = block(dy_ref, at(3, s))
        dys[s] = dy
        back[s] = dot(dy, down_tile(s), ((1,), (1,)))
    fold(prod, 1)
    fold(back, 2)
    for s in range(slots):

        @pl.when(lead[1, s] == s)
        def _():
            act, slope = gelu_parts(prod[s])
            d = d_first[at(1, s)]
            hid[s] = act.astype(BF16)
            dpre[s] = (back[jnp.where(d < 0, slots, d)] * slope).astype(BF16)

    for s in range(slots):
        dp = dpre[lead[1, s]]
        dps[s] = dp
        rprod[s] = dot(dp, up_tile(s), ((1,), (1,)))
        h = first[at(2, s)]
        hs[s] = hid[jnp.where(h < 0, slots, h)]
    fold(rprod, 0)
    for s in range(slots):

        @pl.when(lead[0, s] == s)
        def _():
            r = at(0, s)
            dev, j = r // per_dev, r % per_dev
            to_z, to_core = dev // 2, dev % 2
            k = n_z - 1 - jnp.bitwise_xor(to_z, z) if n_z == 4 else to_z
            whose = jnp.bitwise_xor(to_core, core)
            col = pl.ds(pl.multiple_of(j * TILE, TILE), TILE)
            out[whose * n_z + k, :, col] = rprod[s].astype(BF16)

    for k in range(n_z):
        mine[k][...] = out[k]
        other[k][...] = out[n_z + k]


def relay_kernel(cross, passed, a, b, both, near):
    both[...] = (cross[...].astype(F32) + passed[...].astype(F32)).astype(BF16)
    near[...] = (a[...].astype(F32) + b[...].astype(F32)).astype(BF16)


def add_kernel(a, b, out):
    out[...] = a[...].astype(F32) + b[...].astype(F32)


def main_call(n_f, held, n_z, per_dev, group_cols, place, inputs, cotangent, tiles):
    tok, width = inputs.shape
    slots = n_f * held
    shard = jax.ShapeDtypeStruct((tok, per_dev * TILE), BF16)
    sel = jax.ShapeDtypeStruct((slots, tok, TILE), BF16)
    return pl.pallas_call(
        functools.partial(main_kernel, n_f, held, n_z, per_dev),
        out_shape=[shard] * (2 * n_z) + [sel] * 4,
        in_specs=[SMEM] + [VMEM] * (2 + 2 * n_f),
        out_specs=[VMEM] * (2 * n_z + 4),
        scratch_shapes=[
            pltpu.VMEM((slots, tok, TILE), F32),
            pltpu.VMEM((slots + 1, tok, TILE), F32),
            pltpu.VMEM((slots, tok, TILE), F32),
            pltpu.VMEM((slots + 1, tok, TILE), BF16),
            pltpu.VMEM((slots, tok, TILE), BF16),
            pltpu.VMEM((2 * n_z, tok, per_dev * TILE), BF16),
            pltpu.VMEM((n_f, TILE), jnp.int32),
            pltpu.SMEM((n_f, TILE), jnp.int32),
            pltpu.SMEM((group_cols,), jnp.int32),
            pltpu.SMEM((group_cols,), jnp.int32),
            pltpu.SMEM((width // TILE,), jnp.int32),
            pltpu.SMEM((3, slots), jnp.int32),
            pltpu.SemaphoreType.DMA,
        ],
        compiler_params=vmem_limit(24 if slots <= 16 else 56),
    )(place, inputs, cotangent, *tiles)


def grad_kernel(n_f, held, after, xs, dys, dps, hs, *outs):
    for s in range(n_f * held):
        f, i = s // held, s % held
        out, i = (outs[f % 2], f // 2 * 2 * held + i) if n_f == 4 else (outs[f], i)
        out[i] = dot(xs[s], dps[s], ((0,), (0,))).astype(BF16)
        out[held + i] = dot(hs[s], dys[s], ((0,), (0,))).astype(BF16)


def on_device(inputs, cotangent, up_tiles, up_rows, up_cols, down_tiles, down_rows, down_cols):
    n_f, n_t = lax.axis_size("fsdp"), lax.axis_size("tensor")
    n_z = n_t // 2
    tok, width = inputs.shape
    per_dev = width // (n_t * TILE)
    group_cols = FF // (n_t * TILE)
    held = up_tiles.shape[1]
    rows = held * TILE
    slots = held * n_f
    t = lax.axis_index("tensor")
    z, core = t // 2, t % 2

    zc = jnp.stack([z, core]).astype(jnp.int32)

    def over_f(a, k):
        return lax.ppermute(a, "fsdp", [(f, f ^ k) for f in range(n_f)])

    def over_t(a, k):
        return lax.ppermute(a, "tensor", [(i, i ^ k) for i in range(n_t)])

    up, down = up_tiles[0], down_tiles[0]
    where = (up_rows, up_cols, down_rows, down_cols)
    packed = jax.ShapeDtypeStruct((held * TILE + IDX_ROWS, TILE), BF16)
    downs = [over_f(down, k) for k in range(1, n_f)]
    sent = pl.pallas_call(
        pack_kernel,
        out_shape=packed,
        in_specs=[SMEM] * 4 + [VMEM],
        out_specs=VMEM,
    )(*where, up)
    x_v, dy_v = pl.pallas_call(
        fetch_kernel,
        out_shape=[pltpu.VMEM(inputs.shape, BF16)] * 2,
        in_specs=[HBM, HBM],
        out_specs=[VMEM, VMEM],
        scratch_shapes=[pltpu.SemaphoreType.DMA((2,))],
        compiler_params=vmem_limit(16),
    )(*(pltpu.with_memory_space_constraint(a, pltpu.HBM) for a in (inputs, cotangent)))
    ups = [over_f(sent, k) for k in range(1, n_f)]
    tiles = [sent] + ups + [down] + downs
    outs = main_call(
        n_f, held, n_z, per_dev, group_cols, zc, x_v, dy_v, tiles
    )
    mine, other = outs[:n_z], outs[n_z : 2 * n_z]
    chosen = outs[2 * n_z :]
    def joined(q, lo=0, hi=None):
        a, b = mine[q][:, lo:hi], theirs[q][:, lo:hi]
        return (a.astype(F32) + b.astype(F32)).astype(BF16)

    theirs = [over_t(o, 1) for o in other]
    if n_z == 4:
        cut = per_dev * TILE * 5 // 8
        op_a = joined(0, 0, cut)
        passed = over_t(op_a, 2)
        op_b = joined(0, cut)
        passed2 = over_t(op_b, 2)
        across = over_t((joined(1, 0, cut).astype(F32) + passed.astype(F32)).astype(BF16), 4)
        both, near = pl.pallas_call(
            relay_kernel,
            out_shape=[
                jax.ShapeDtypeStruct(passed2.shape, BF16),
                jax.ShapeDtypeStruct(mine[2].shape, BF16),
            ],
            in_specs=[VMEM] * 4,
            out_specs=[VMEM] * 2,
            compiler_params=vmem_limit(8),
        )(joined(1, cut), passed2, mine[2], theirs[2])
        across2 = over_t(both, 4)
        came = over_t(near, 2)
        own = joined(3)
        acc = pl.pallas_call(
            add_kernel,
            out_shape=jax.ShapeDtypeStruct(own.shape, F32),
            in_specs=[VMEM] * 2,
            out_specs=VMEM,
            compiler_params=vmem_limit(8),
        )(own, came)
        input_grad = jnp.concatenate(
            [(acc[:, :cut] + across.astype(F32)).astype(BF16), (acc[:, cut:] + across2.astype(F32)).astype(BF16)], axis=1
        )
        gate = op_a
    else:
        input_grad = lax.psum_scatter(
            jnp.stack([joined(q) for q in range(n_z)]),
            "tensor",
            scatter_dimension=0,
            tiled=False,
            axis_index_groups=[list(range(c, n_t, 2)) for c in range(2)],
        )
        gate = theirs[0]
    sets = 2 if n_f == 4 else n_f
    terms = pl.pallas_call(
        functools.partial(grad_kernel, n_f, held),
        out_shape=[jax.ShapeDtypeStruct((n_f // sets * 2 * held, TILE, TILE), BF16)] * sets,
        in_specs=[ANY] + [VMEM] * 4,
        out_specs=[VMEM] * sets,
        compiler_params=vmem_limit(16),
    )(gate, *chosen)
    if n_f == 4:
        half = terms[0].astype(F32) + over_f(terms[1], 1).astype(F32)
        total = half[: 2 * held] + over_f(half[2 * held :].astype(BF16), 2).astype(F32)
    else:
        total = terms[0].astype(F32)
        for k in range(1, n_f):
            total = total + over_f(terms[k], k).astype(F32)
    total = total.astype(BF16)
    return (input_grad, total[:held][None], total[held:][None])


def solution(mesh):
    placed = (
        P("fsdp", None),
        P("fsdp", None),
        P("tensor", "fsdp", None, None),
        P("tensor", "fsdp"),
        P("tensor", "fsdp"),
        P("tensor", "fsdp", None, None),
        P("tensor", "fsdp"),
        P("tensor", "fsdp"),
    )
    return jax.shard_map(
        on_device,
        mesh=mesh,
        in_specs=placed,
        out_specs=(
            P("fsdp", "tensor"),
            P("tensor", "fsdp", None, None),
            P("tensor", "fsdp", None, None),
        ),
        check_vma=False,
    )
```
